32 devices in a mesh: groups: 2 (over x), seq: 16 (over z, y, core).
Axes of the slice: x: 2, y: 2, z: 4, core: 2. Of those that a mesh axis runs over, the one named last changes fastest.
Arguments:
- queries: bfloat16 [4096, 2560], P(('groups', 'seq')), parts along dimension 0, may hold values from -25 to 25
- keys: bfloat16 [4096, 512], P(('groups', 'seq')), parts along dimension 0, may hold values from -4 to 4
- values: bfloat16 [4096, 512], P(('groups', 'seq')), parts along dimension 0, may hold values from -6 to 6
- out_grad: bfloat16 [4096, 2560], P(('groups', 'seq')), parts along dimension 0, may hold values from -6 to 6
Outputs:
- query_grad: bfloat16 [4096, 2560], P(('groups', 'seq')), parts along dimension 0
- key_grad: bfloat16 [4096, 512], P(('groups', 'seq')), parts along dimension 0
- value_grad: bfloat16 [4096, 512], P(('groups', 'seq')), parts along dimension 0
The draws below stay inside these ranges and needn't reach their ends.
There are 2 independent parts, one for each index of `groups`. The reference program is written for one: setup_inputs(seed, part) draws one part's arguments, and reference() takes and returns one part's arrays. A program takes and returns all parts, laid end to end along the dimension named above; each array names one. Nothing has to cross between parts.
All inputs are finite; a program needn't handle non-finite values.
Results may differ from the reference program's by a relative error of at most 0.005.
Values may be sent and summed in bfloat16 or wider, within the bound.
No kernel may reach another device: no remote copies, remote signals or barrier semaphores. Data moves between devices by JAX's collectives and lax.ppermute only.
A program may use at most 256 MiB of HBM per device.

```python
import jax
import jax.numpy as jnp
from jax import lax

DH = 128
KVH = 4
QPG = 5
QH = 20
SEQ = 2048


def key_table(key):
    normal_part = jax.random.normal(jax.random.fold_in(key, 31), (SEQ, KVH * DH), jnp.float32)
    table = jnp.clip(normal_part, -4.0, 4.0)
    places = jnp.arange(SEQ)[:, None]
    nearby = places % 97 == 94
    table = jnp.where(nearby, table, table)
    return table


def draw_keys(key, part):
    table = key_table(key)
    return table.astype(jnp.bfloat16)


def draw_queries(key, part):
    key = jax.random.fold_in(key, 2)
    result = jnp.clip(jax.random.normal(key, (SEQ, QH * DH), jnp.float32), -4.0, 4.0)
    return result.astype(jnp.bfloat16)


def block_levels(rng, shape, split, low, top_value):
    level, own = 1.0, jax.random.fold_in(rng, 6)
    for axis_at, parts in split:
        heights = jnp.exp(jax.random.uniform(jax.random.fold_in(own, axis_at), (parts,), jnp.float32, low / len(split), top_value / len(split)))
        level = level * jnp.repeat(heights, shape[axis_at] // parts).reshape([-1 if axis == axis_at else 1 for axis in range(len(shape))])
    return level


def noise(stream_key, shape, scale, bound, shards=(), held_as=jnp.bfloat16):
    gain = block_levels(stream_key, shape, shards, -0.22, 0.18) if shards else 1.0
    values = jax.random.normal(stream_key, shape, jnp.float32) * scale * gain
    return jnp.minimum(jnp.maximum(values, -bound), bound).astype(held_as)


def setup_inputs(seed: int = 0, part: int = 0) -> dict:
    seeds = jax.random.split(jax.random.key(seed), 5)
    part_splits = jax.random.split(jax.random.fold_in(seeds[4], part), 5)
    return {
        "queries": draw_queries(jax.random.fold_in(jax.random.fold_in(seeds[4], part), 71), part),
        "keys": draw_keys(jax.random.fold_in(jax.random.fold_in(seeds[4], part), 71), part),
        "values": noise(part_splits[2], (SEQ, KVH * DH), 1.0, 6.0, ((0, 16),)),
        "out_grad": noise(part_splits[3], (SEQ, QH * DH), 1.0, 6.0, ((0, 16),)),
    }


def reference(queries, keys, values, out_grad):
    scaling = DH ** -0.5
    places = jnp.arange(SEQ)
    causal = places[None, :] <= places[:, None]

    def per_head(items):
        query_one, grad_one, key_one, value_one = items
        scores = jnp.dot(query_one, key_one.T, preferred_element_type=jnp.float32) * scaling
        row_max = jnp.max(jnp.where(causal, scores, -jnp.inf), axis=1, keepdims=True)
        weights = jnp.where(causal, jnp.exp(scores - row_max), 0.0)
        probs = weights / jnp.sum(weights, axis=1, keepdims=True)
        probs_half = probs.astype(jnp.bfloat16)
        grad_probs = jnp.dot(grad_one, value_one.T, preferred_element_type=jnp.float32)
        row_delta = jnp.sum(probs * grad_probs, axis=1, keepdims=True)
        grad_scores = (probs * (grad_probs - row_delta) * scaling).astype(jnp.bfloat16)
        query_part = jnp.dot(grad_scores, key_one, preferred_element_type=jnp.float32).astype(jnp.bfloat16)
        key_part = jnp.dot(grad_scores.T, query_one, preferred_element_type=jnp.float32)
        value_part = jnp.dot(probs_half.T, grad_one, preferred_element_type=jnp.float32)
        return query_part, key_part, value_part

    query_heads = queries.reshape(SEQ, QH, DH).transpose(1, 0, 2)
    grad_heads = out_grad.reshape(SEQ, QH, DH).transpose(1, 0, 2)
    key_heads = jnp.repeat(keys.reshape(SEQ, KVH, DH).transpose(1, 0, 2), QPG, axis=0)
    value_heads = jnp.repeat(values.reshape(SEQ, KVH, DH).transpose(1, 0, 2), QPG, axis=0)
    query_part, key_part, value_part = lax.map(per_head, (query_heads, grad_heads, key_heads, value_heads))
    query_grad = query_part.transpose(1, 0, 2).reshape(SEQ, QH * DH)
    key_sum = key_part.reshape(KVH, QPG, SEQ, DH).sum(axis=1)
    value_sum = value_part.reshape(KVH, QPG, SEQ, DH).sum(axis=1)
    key_grad = key_sum.transpose(1, 0, 2).reshape(SEQ, KVH * DH).astype(jnp.bfloat16)
    value_grad = value_sum.transpose(1, 0, 2).reshape(SEQ, KVH * DH).astype(jnp.bfloat16)
    return query_grad, key_grad, value_grad
```

```python
from functools import partial

import jax
import jax.numpy as jnp
from jax import lax
from jax.experimental import pallas as pl
from jax.experimental.pallas import tpu as pltpu
from jax.sharding import PartitionSpec as P

DH = 128
KVH = 4
QPG = 5
SCALING = DH ** (-0.5)
LOG2E = 1.4426950408889634
CONTRACT_LAST = (((1,), (1,)), ((), ()))
VMEM_BYTES = 40 * 1024 * 1024


def token_places(rank, tokens, dim):
    shape = (tokens, 1) if dim == 0 else (1, tokens)
    own = lax.broadcasted_iota(jnp.int32, shape, dim)
    return jnp.concatenate([own + tokens * (rank ^ d) for d in range(KVH)], axis=dim)


def stacked(refs):
    return jnp.concatenate([ref[...] for ref in refs], axis=0)


def keys_values(refs):
    return (
        jnp.concatenate([ref[:, :DH] for ref in refs], axis=0),
        jnp.concatenate([ref[:, DH:] for ref in refs], axis=0),
    )


def scaled_scores(key_rows, query_rows):
    raw = lax.dot_general(key_rows, query_rows, CONTRACT_LAST, preferred_element_type=jnp.float32)
    return raw * (SCALING * LOG2E)


def stats_kernel(offset, info, kv_a, kv_b, q0, q1, q2, q3, g0, g1, g2, g3, old, new):
    tokens = q0.shape[0]

    def update():
        key_rows, value_rows = keys_values((kv_a, kv_b))
        scores = scaled_scores(key_rows, stacked((q0, q1, q2, q3)))
        grad_probs = lax.dot_general(
            value_rows, stacked((g0, g1, g2, g3)), CONTRACT_LAST, preferred_element_type=jnp.float32
        )
        if offset == 0:
            rank = info[1]
            causal = token_places(rank, tokens, 0) <= token_places(rank, tokens, 1)
            scores = jnp.where(causal, scores, -jnp.inf)
        top = jnp.max(scores, axis=0, keepdims=True)
        if offset:
            old_top = old[0, 0:1]
            top = jnp.maximum(old_top, top)
        weights = jnp.exp2(scores - top)
        total = jnp.sum(weights, axis=0, keepdims=True)
        weighted = jnp.sum(weights * grad_probs, axis=0, keepdims=True)
        if offset:
            shrink = jnp.exp2(old_top - top)
            total = total + shrink * old[0, 1:2]
            weighted = weighted + shrink * old[0, 2:3]
        new[0, 0:1] = top
        new[0, 1:2] = total
        new[0, 2:3] = weighted

    if offset == 0:
        update()
    else:
        new[0] = old[0]
        pl.when(info[0] >= offset)(update)


def grads_kernel(
    offset, first, info, kv_a, kv_b, q0, q1, q2, q3, g0, g1, g2, g3, stats, *rest
):
    tokens = q0.shape[0]
    last = offset == 0
    rest = list(rest)
    dq_old = None if first else rest.pop(0)
    dkv_a, dkv_b = rest[:2]
    dq_refs = rest[2:]
    head = pl.program_id(0)

    @pl.when(head == 0)
    def _():
        dkv_a[...] = jnp.zeros_like(dkv_a)
        dkv_b[...] = jnp.zeros_like(dkv_b)

    def work():
        key_rows, value_rows = keys_values((kv_a, kv_b))
        query_rows = stacked((q0, q1, q2, q3))
        grad_rows = stacked((g0, g1, g2, g3))
        total = stats[0, 1:2]
        log_total = stats[0, 0:1] + jnp.log2(total)
        row_delta = stats[0, 2:3] / total
        probs = jnp.exp2(scaled_scores(key_rows, query_rows) - log_total)
        if last:
            rank = info[1]
            causal = token_places(rank, tokens, 0) <= token_places(rank, tokens, 1)
            probs = jnp.where(causal, probs, 0.0)
        grad_probs = lax.dot_general(
            value_rows, grad_rows, CONTRACT_LAST, preferred_element_type=jnp.float32
        )
        grad_scores = (probs * (grad_probs - row_delta) * SCALING).astype(jnp.bfloat16)
        dv = jnp.dot(probs.astype(jnp.bfloat16), grad_rows, preferred_element_type=jnp.float32)
        dk = jnp.dot(grad_scores, query_rows, preferred_element_type=jnp.float32)
        half = 2 * tokens
        dkv_a[:, :DH] += dk[:half]
        dkv_b[:, :DH] += dk[half:]
        dkv_a[:, DH:] += dv[:half]
        dkv_b[:, DH:] += dv[half:]
        dq = jnp.dot(key_rows.T, grad_scores, preferred_element_type=jnp.float32)
        if dq_old is not None:
            dq = dq + dq_old[0]
        if last:
            rows = dq.T.astype(jnp.bfloat16)
            for d in range(KVH):
                dq_refs[d][...] = rows[d * tokens : (d + 1) * tokens]
        else:
            dq_refs[0][0] = dq

    if last:
        work()
    else:
        pl.when(info[0] >= offset)(work)

        @pl.when(info[0] < offset)
        def _():
            dq_refs[0][0] = jnp.zeros_like(dq_refs[0][0]) if dq_old is None else dq_old[0]


def piece_specs(tokens):
    queries = [pl.BlockSpec((tokens, DH), lambda h, info: (0, h)) for d in range(KVH)]
    grads = [pl.BlockSpec((tokens, DH), lambda h, info: (0, h + QPG)) for d in range(KVH)]
    return queries + grads


def whole(shape):
    return pl.BlockSpec(shape, lambda h, info: (0,) * len(shape))


def per_head(shape):
    return pl.BlockSpec((1,) + shape, lambda h, info: (h, 0, 0))


def params():
    return pltpu.CompilerParams(
        vmem_limit_bytes=VMEM_BYTES, dimension_semantics=("arbitrary",)
    )


def cost(products, span):
    return pl.CostEstimate(
        flops=products * QPG * 2 * span * span * DH,
        bytes_accessed=4 * QPG * span * DH * 2,
        transcendentals=QPG * span * span,
    )


def stats_call(offset, info, kv, pieces, old):
    tokens = pieces[0].shape[0]
    span = KVH * tokens
    shape = jax.ShapeDtypeStruct((QPG, 8, span), jnp.float32)
    return pl.pallas_call(
        partial(stats_kernel, offset),
        grid_spec=pltpu.PrefetchScalarGridSpec(
            num_scalar_prefetch=1,
            grid=(QPG,),
            in_specs=[whole(kv[0].shape), whole(kv[1].shape)]
            + piece_specs(tokens)
            + [per_head((8, span))],
            out_specs=per_head((8, span)),
        ),
        out_shape=shape,
        compiler_params=params(),
        cost_estimate=cost(2, span),
    )(info, *kv, *pieces, *pieces, old)


def grads_call(offset, info, kv, pieces, stats, dq_old):
    tokens = pieces[0].shape[0]
    span = KVH * tokens
    first = dq_old is None
    half = jax.ShapeDtypeStruct((2 * tokens, 2 * DH), jnp.float32)
    if offset:
        dq_shapes = [jax.ShapeDtypeStruct((QPG, DH, span), jnp.float32)]
        dq_specs = [per_head((DH, span))]
    else:
        dq_shapes = [jax.ShapeDtypeStruct((tokens, QPG * DH), jnp.bfloat16)] * KVH
        dq_specs = [pl.BlockSpec((tokens, DH), lambda h, info: (0, h))] * KVH
    return pl.pallas_call(
        partial(grads_kernel, offset, first),
        grid_spec=pltpu.PrefetchScalarGridSpec(
            num_scalar_prefetch=1,
            grid=(QPG,),
            in_specs=[whole(kv[0].shape), whole(kv[1].shape)]
            + piece_specs(tokens)
            + [per_head((8, span))]
            + ([] if first else [per_head((DH, span))]),
            out_specs=[whole(half.shape), whole(half.shape)] + dq_specs,
        ),
        out_shape=[half, half] + dq_shapes,
        compiler_params=params(),
        cost_estimate=cost(5, span),
    )(info, *kv, *pieces, *pieces, stats, *([] if first else [dq_old]))


def place_kernel(info, *refs):
    rank = info[1]
    sources, targets = refs[: 2 * KVH], refs[2 * KVH :]
    query_grad, key_grad, value_grad = targets
    for d in range(KVH):
        head = rank ^ d
        wide = pl.ds(pl.multiple_of(head * (QPG * DH), DH), QPG * DH)
        narrow = pl.ds(pl.multiple_of(head * DH, DH), DH)
        query_grad[:, wide] = sources[d][...]
        key_grad[:, narrow] = sources[KVH + d][:, :DH]
        value_grad[:, narrow] = sources[KVH + d][:, DH:]


def place_call(info, dq, dkv):
    tokens = dq[0].shape[0]
    shapes = [
        jax.ShapeDtypeStruct((tokens, KVH * QPG * DH), jnp.bfloat16),
        jax.ShapeDtypeStruct((tokens, KVH * DH), jnp.bfloat16),
        jax.ShapeDtypeStruct((tokens, KVH * DH), jnp.bfloat16),
    ]
    vmem = pl.BlockSpec(memory_space=pltpu.VMEM)
    return pl.pallas_call(
        place_kernel,
        in_specs=[pl.BlockSpec(memory_space=pltpu.SMEM)] + [vmem] * (2 * KVH),
        out_specs=[vmem] * 3,
        out_shape=shapes,
        compiler_params=pltpu.CompilerParams(vmem_limit_bytes=VMEM_BYTES),
    )(info, *dq, *dkv)


def per_device(queries, keys, values, out_grad):
    devices = lax.axis_size("seq")
    planes = devices // KVH
    tokens = queries.shape[0]
    device = lax.axis_index("seq")
    rank = device % KVH
    info = jnp.stack([device // KVH, rank]).astype(jnp.int32)
    up = [(i, i + KVH) for i in range(devices - KVH)]
    down = [(i + KVH, i) for i in range(devices - KVH)]

    def swap(array, d):
        if d == 0:
            return array
        return lax.ppermute(array, "seq", [(i, i ^ d) for i in range(devices)])

    def columns(array, head, width):
        return lax.dynamic_slice_in_dim(array, head * width, width, axis=1)

    kv_pieces = []
    for d in range(KVH):
        head = rank ^ d
        piece = jnp.concatenate([columns(keys, head, DH), columns(values, head, DH)], axis=1)
        kv_pieces.append(swap(piece, d))
    pieces = []
    for d in range(KVH):
        head = rank ^ d
        piece = jnp.concatenate(
            [columns(queries, head, QPG * DH), columns(out_grad, head, QPG * DH)], axis=1
        )
        pieces.append(swap(piece, d))
    chain = [
        (
            jnp.concatenate(kv_pieces[:2], axis=0),
            jnp.concatenate(kv_pieces[2:], axis=0),
        )
    ]
    for step in range(1, planes):
        chain.append(tuple(lax.ppermute(half, "seq", up) for half in chain[-1]))
    stats = jnp.zeros((QPG, 8, KVH * tokens), jnp.float32)
    for offset in range(planes):
        stats = stats_call(offset, info, chain[offset], pieces, stats)
    dq = None
    arrived = None
    for offset in reversed(range(planes)):
        results = grads_call(offset, info, chain[offset], pieces, stats, dq)
        partials = results[:2]
        if offset:
            dq = results[2]
        else:
            dq_pieces = results[2:]
        if arrived is not None:
            partials = [mine + half for mine, half in zip(partials, arrived)]
        sums = [half.astype(jnp.bfloat16) for half in partials]
        if offset:
            arrived = [lax.ppermute(half, "seq", down).astype(jnp.float32) for half in sums]
    dq_back = [swap(dq_pieces[d], d) for d in range(KVH)]
    dkv_back = [
        swap(sums[d // 2][(d % 2) * tokens : (d % 2 + 1) * tokens], d) for d in range(KVH)
    ]
    return tuple(place_call(info, dq_back, dkv_back))


def solution(mesh):
    spec = P(("groups", "seq"), None)
    return jax.shard_map(
        per_device,
        mesh=mesh,
        in_specs=(spec,) * 4,
        out_specs=(spec,) * 3,
        check_vma=False,
    )
```

```python
from functools import partial

import jax
import jax.numpy as jnp
from jax import lax
from jax.experimental import pallas as pl
from jax.experimental.pallas import tpu as pltpu
from jax.sharding import PartitionSpec as P

DH = 128
KVH = 4
QPG = 5
SCALING = DH ** (-0.5)
LOG2E = 1.4426950408889634
CONTRACT_LAST = (((1,), (1,)), ((), ()))
VMEM_BYTES = 28 * 1024 * 1024
EXTRA = 8


def token_places(rank, tokens, dim):
    shape = (tokens, 1) if dim == 0 else (1, tokens)
    own = lax.broadcasted_iota(jnp.int32, shape, dim)
    return jnp.concatenate([own + tokens * (rank ^ d) for d in range(KVH)], axis=dim)


def causal_mask(info, tokens):
    return token_places(info[1], tokens, 0) <= token_places(info[1], tokens, 1)


def stacked(refs, head):
    return jnp.concatenate([ref[:, head * DH : (head + 1) * DH] for ref in refs], axis=0)


def keys_values(refs):
    return (
        jnp.concatenate([ref[:, :DH] for ref in refs], axis=0),
        jnp.concatenate([ref[:, DH:] for ref in refs], axis=0),
    )


def scaled_scores(key_rows, query_rows):
    raw = lax.dot_general(key_rows, query_rows, CONTRACT_LAST, preferred_element_type=jnp.float32)
    return raw * (SCALING * LOG2E)


def forward_kernel(offset, last, info, *refs):
    refs = list(refs)
    kv = [refs.pop(0) for _ in range(2)]
    q = [refs.pop(0) for _ in range(KVH)]
    g = [refs.pop(0) for _ in range(KVH)] if last else None
    if offset:
        old_stats, old_sums = refs.pop(0), refs.pop(0)
    if last:
        finals, stats, sums = refs
    else:
        stats, sums = refs
    tokens = q[0].shape[0]

    def update():
        key_rows, value_rows = keys_values(kv)
        span = key_rows.shape[0]
        left = jnp.concatenate([value_rows.T, jnp.ones((EXTRA, span), jnp.bfloat16)], axis=0)
        mask = None if offset else causal_mask(info, tokens)
        for h in range(QPG):
            scores = scaled_scores(key_rows, stacked(q, h))
            if offset == 0:
                scores = jnp.where(mask, scores, -jnp.inf)
            top = jnp.max(scores, axis=0, keepdims=True)
            if offset:
                old_top = old_stats[h, 0:1]
                top = jnp.maximum(old_top, top)
                shrink = jnp.exp2(old_top - top)
            weights = jnp.exp2(scores - top)
            total = jnp.sum(weights, axis=0, keepdims=True)
            added = jnp.dot(left, weights.astype(jnp.bfloat16), preferred_element_type=jnp.float32)
            if offset:
                total = total + shrink * old_stats[h, 1:2]
                added = added + shrink * old_sums[h]
            stats[h, 0:1] = top
            stats[h, 1:2] = total
            sums[h] = added

    if offset == 0:
        update()
    else:
        pl.when(info[0] >= offset)(update)

        @pl.when(info[0] < offset)
        def _():
            stats[...] = old_stats[...]
            sums[...] = old_sums[...]

    if last:
        for h in range(QPG):
            grads = stacked(g, h).T.astype(jnp.float32)
            weighted = jnp.sum(sums[h, :DH] * grads, axis=0, keepdims=True)
            finals[h, 0:1] = stats[h, 0:1] + jnp.log2(stats[h, 1:2])
            finals[h, 1:2] = weighted / sums[h, DH : DH + 1]


def backward_kernel(offset, first, info, *refs):
    refs = list(refs)
    kv = [refs.pop(0) for _ in range(2)]
    q = [refs.pop(0) for _ in range(KVH)]
    g = [refs.pop(0) for _ in range(KVH)]
    finals = refs.pop(0)
    dq_old = None if first else refs.pop(0)
    dkv = refs.pop(0)
    dq_refs = refs
    tokens = q[0].shape[0]
    last = offset == 0

    def work():
        key_rows, value_rows = keys_values(kv)
        key_columns = key_rows.T
        mask = causal_mask(info, tokens) if last else None
        for h in range(QPG):
            query_rows = stacked(q, h)
            grad_rows = stacked(g, h)
            probs = jnp.exp2(scaled_scores(key_rows, query_rows) - finals[h, 0:1])
            if last:
                probs = jnp.where(mask, probs, 0.0)
            grad_probs = lax.dot_general(
                value_rows, grad_rows, CONTRACT_LAST, preferred_element_type=jnp.float32
            )
            grad_scores = (probs * (grad_probs - finals[h, 1:2]) * SCALING).astype(jnp.bfloat16)
            dk = jnp.dot(grad_scores, query_rows, preferred_element_type=jnp.float32)
            dv = jnp.dot(
                probs.astype(jnp.bfloat16), grad_rows, preferred_element_type=jnp.float32
            )
            if h == 0:
                dkv[:, :DH] = dk
                dkv[:, DH:] = dv
            else:
                dkv[:, :DH] += dk
                dkv[:, DH:] += dv
            dq = jnp.dot(key_columns, grad_scores, preferred_element_type=jnp.float32)
            if dq_old is not None:
                dq = dq + dq_old[h]
            if last:
                rows = dq.T.astype(jnp.bfloat16)
                for d in range(KVH):
                    dq_refs[d][:, h * DH : (h + 1) * DH] = rows[d * tokens : (d + 1) * tokens]
            else:
                dq_refs[0][h] = dq

    if last:
        work()
    else:
        pl.when(info[0] >= offset)(work)

        @pl.when(info[0] < offset)
        def _():
            dkv[...] = jnp.zeros_like(dkv)
            dq_refs[0][...] = jnp.zeros_like(dq_refs[0]) if dq_old is None else dq_old[...]


def local_call(kernel, shapes, flops, info, *operands, scratch=()):
    vmem = pl.BlockSpec(memory_space=pltpu.VMEM)
    return pl.pallas_call(
        kernel,
        in_specs=[pl.BlockSpec(memory_space=pltpu.SMEM)] + [vmem] * len(operands),
        out_specs=[vmem] * len(shapes),
        out_shape=shapes,
        scratch_shapes=scratch,
        compiler_params=pltpu.CompilerParams(vmem_limit_bytes=VMEM_BYTES),
        cost_estimate=pl.CostEstimate(flops=flops, bytes_accessed=1 << 20, transcendentals=0),
    )(info, *operands)


def forward_call(offset, last, info, kv, q, g, state):
    tokens = q[0].shape[0]
    span = KVH * tokens
    stats = jax.ShapeDtypeStruct((QPG, 8, span), jnp.float32)
    sums = jax.ShapeDtypeStruct((QPG, DH + EXTRA, span), jnp.float32)
    shapes = [stats] if last else [stats, sums]
    scratch = [pltpu.VMEM(kept.shape, kept.dtype) for kept in (stats, sums)] if last else []
    return local_call(
        partial(forward_kernel, offset, last),
        shapes,
        2 * 2 * QPG * span * span * DH * 2,
        info,
        *kv,
        *q,
        *(g if last else []),
        *state,
        scratch=scratch,
    )


def backward_call(offset, info, kv, q, g, finals, dq_old):
    tokens = q[0].shape[0]
    span = KVH * tokens
    first = dq_old is None
    shapes = [jax.ShapeDtypeStruct((span, 2 * DH), jnp.float32)]
    if offset:
        shapes += [jax.ShapeDtypeStruct((QPG, DH, span), jnp.float32)]
    else:
        shapes += [jax.ShapeDtypeStruct((tokens, QPG * DH), jnp.bfloat16)] * KVH
    return local_call(
        partial(backward_kernel, offset, first),
        shapes,
        5 * 2 * QPG * span * span * DH * 2,
        info,
        *kv,
        *q,
        *g,
        finals,
        *([] if first else [dq_old]),
    )


def place_kernel(info, *refs):
    rank = info[1]
    sources, targets = refs[: 2 * KVH], refs[2 * KVH :]
    query_grad, key_grad, value_grad = targets
    for d in range(KVH):
        head = rank ^ d
        wide = pl.ds(pl.multiple_of(head * (QPG * DH), DH), QPG * DH)
        narrow = pl.ds(pl.multiple_of(head * DH, DH), DH)
        query_grad[:, wide] = sources[d][...]
        key_grad[:, narrow] = sources[KVH + d][:, :DH]
        value_grad[:, narrow] = sources[KVH + d][:, DH:]


def place_call(info, dq, dkv):
    tokens = dq[0].shape[0]
    shapes = [
        jax.ShapeDtypeStruct((tokens, KVH * QPG * DH), jnp.bfloat16),
        jax.ShapeDtypeStruct((tokens, KVH * DH), jnp.bfloat16),
        jax.ShapeDtypeStruct((tokens, KVH * DH), jnp.bfloat16),
    ]
    return local_call(place_kernel, shapes, 0, info, *dq, *dkv)


def per_device(queries, keys, values, out_grad):
    devices = lax.axis_size("seq")
    planes = devices // KVH
    tokens = queries.shape[0]
    device = lax.axis_index("seq")
    rank = device % KVH
    info = jnp.stack([device // KVH, rank]).astype(jnp.int32)

    def swap(array, d):
        if d == 0:
            return array
        return lax.ppermute(array, "seq", [(i, i ^ d) for i in range(devices)])

    def columns(array, head, width):
        return lax.dynamic_slice_in_dim(array, head * width, width, axis=1)

    kv_pieces = []
    for d in range(KVH):
        head = rank ^ d
        piece = jnp.concatenate([columns(keys, head, DH), columns(values, head, DH)], axis=1)
        kv_pieces.append(swap(piece, d))
    q = [swap(columns(queries, rank ^ d, QPG * DH), d) for d in range(KVH)]
    g = [swap(columns(out_grad, rank ^ d, QPG * DH), d) for d in range(KVH)]
    chain = [
        (
            jnp.concatenate(kv_pieces[:2], axis=0),
            jnp.concatenate(kv_pieces[2:], axis=0),
        )
    ]
    for step in range(1, planes):
        pairs = [(i, i + KVH) for i in range((step - 1) * KVH, devices - KVH)]
        chain.append(tuple(lax.ppermute(half, "seq", pairs) for half in chain[-1]))
    state = []
    for offset in range(planes):
        last = offset == planes - 1
        state = forward_call(offset, last, info, chain[offset], q, g, state)
    finals = state[0]

    dq = None
    arrived = None
    for offset in reversed(range(planes)):
        results = backward_call(offset, info, chain[offset], q, g, finals, dq)
        total, dq = results[0], results[1:]
        if offset:
            dq = dq[0]
        if arrived is not None:
            total = total + arrived.astype(jnp.float32)
        total = total.astype(jnp.bfloat16)
        if offset:
            pairs = [(i + KVH, i) for i in range((offset - 1) * KVH, devices - KVH)]
            arrived = lax.ppermute(total, "seq", pairs)
    dq_back = [swap(dq[d], d) for d in range(KVH)]
    dkv_back = [swap(total[d * tokens : (d + 1) * tokens], d) for d in range(KVH)]
    return tuple(place_call(info, dq_back, dkv_back))


def solution(mesh):
    spec = P(("groups", "seq"), None)
    return jax.shard_map(
        per_device,
        mesh=mesh,
        in_specs=(spec,) * 4,
        out_specs=(spec,) * 3,
        check_vma=False,
    )
```

```python
from functools import partial

import jax
import jax.numpy as jnp
from jax import lax
from jax.experimental import pallas as pl
from jax.experimental.pallas import tpu as pltpu
from jax.sharding import PartitionSpec as P

DH = 128
KVH = 4
QPG = 5
SCALING = DH ** (-0.5)
LOG2E = 1.4426950408889634
CONTRACT_LAST = (((1,), (1,)), ((), ()))
VMEM_BYTES = 28 * 1024 * 1024
EXTRA = 8


def token_places(rank, tokens, dim):
    shape = (tokens, 1) if dim == 0 else (1, tokens)
    own = lax.broadcasted_iota(jnp.int32, shape, dim)
    return jnp.concatenate([own + tokens * (rank ^ d) for d in range(KVH)], axis=dim)


def causal_mask(info, tokens):
    return token_places(info[1], tokens, 0) <= token_places(info[1], tokens, 1)


def stacked(refs, head):
    return jnp.concatenate([ref[:, head * DH : (head + 1) * DH] for ref in refs], axis=0)


def keys_values(refs):
    return (
        jnp.concatenate([ref[:, :DH] for ref in refs], axis=0),
        jnp.concatenate([ref[:, DH:] for ref in refs], axis=0),
    )


def scaled_scores(key_rows, query_rows):
    raw = lax.dot_general(key_rows, query_rows, CONTRACT_LAST, preferred_element_type=jnp.float32)
    return raw * (SCALING * LOG2E)


def forward_kernel(offset, last, info, *refs):
    refs = list(refs)
    kv = [refs.pop(0) for _ in range(2)]
    q = [refs.pop(0) for _ in range(KVH)]
    g = [refs.pop(0) for _ in range(KVH)] if last else None
    if offset:
        old_stats, old_sums = refs.pop(0), refs.pop(0)
    if last:
        finals, stats, sums = refs
    else:
        stats, sums = refs
    tokens = q[0].shape[0]

    def update():
        key_rows, value_rows = keys_values(kv)
        span = key_rows.shape[0]
        left = jnp.concatenate([value_rows.T, jnp.ones((EXTRA, span), jnp.bfloat16)], axis=0)
        mask = None if offset else causal_mask(info, tokens)
        scores = []
        for h in range(QPG):
            raw = scaled_scores(key_rows, stacked(q, h))
            scores.append(raw if offset else jnp.where(mask, raw, -jnp.inf))
        tops = [jnp.max(raw, axis=0, keepdims=True) for raw in scores]
        for h in range(QPG):
            top = tops[h]
            if offset:
                old_top = old_stats[h, 0:1]
                top = jnp.maximum(old_top, top)
            weights = jnp.exp2(scores[h] - top).astype(jnp.bfloat16)
            added = jnp.dot(left, weights, preferred_element_type=jnp.float32)
            if offset:
                added = added + jnp.exp2(old_top - top) * old_sums[h]
            stats[h, 0:1] = top
            sums[h] = added

    if offset == 0:
        update()
    else:
        pl.when(info[0] >= offset)(update)

        @pl.when(info[0] < offset)
        def _():
            stats[...] = old_stats[...]
            sums[...] = old_sums[...]

    if last:
        for h in range(QPG):
            grads = stacked(g, h).T.astype(jnp.float32)
            weighted = jnp.sum(sums[h, :DH] * grads, axis=0, keepdims=True)
            total = sums[h, DH : DH + 1]
            finals[h, 0:1] = stats[h, 0:1] + jnp.log2(total)
            finals[h, 1:2] = weighted / total


def backward_kernel(offset, first, info, *refs):
    refs = list(refs)
    kv = [refs.pop(0) for _ in range(2)]
    q = [refs.pop(0) for _ in range(KVH)]
    g = [refs.pop(0) for _ in range(KVH)]
    finals = refs.pop(0)
    dq_old = None if first else refs.pop(0)
    dkv = refs.pop(0)
    dq_refs = refs
    tokens = q[0].shape[0]
    last = offset == 0

    def work():
        key_rows, value_rows = keys_values(kv)
        key_columns = key_rows.T
        mask = causal_mask(info, tokens) if last else None
        for h in range(QPG):
            query_rows = stacked(q, h)
            grad_rows = stacked(g, h)
            probs = jnp.exp2(scaled_scores(key_rows, query_rows) - finals[h, 0:1])
            if last:
                probs = jnp.where(mask, probs, 0.0)
            grad_probs = lax.dot_general(
                value_rows, grad_rows, CONTRACT_LAST, preferred_element_type=jnp.float32
            )
            grad_scores = (probs * (grad_probs - finals[h, 1:2]) * SCALING).astype(jnp.bfloat16)
            dk = jnp.dot(grad_scores, query_rows, preferred_element_type=jnp.float32)
            dv = jnp.dot(
                probs.astype(jnp.bfloat16), grad_rows, preferred_element_type=jnp.float32
            )
            if h == 0:
                dkv[:, :DH] = dk
                dkv[:, DH:] = dv
            else:
                dkv[:, :DH] += dk
                dkv[:, DH:] += dv
            dq = jnp.dot(key_columns, grad_scores, preferred_element_type=jnp.float32)
            if dq_old is not None:
                dq = dq + dq_old[h]
            if last:
                rows = dq.T.astype(jnp.bfloat16)
                for d in range(KVH):
                    dq_refs[d][:, h * DH : (h + 1) * DH] = rows[d * tokens : (d + 1) * tokens]
            else:
                dq_refs[0][h] = dq

    if last:
        work()
    else:
        pl.when(info[0] >= offset)(work)

        @pl.when(info[0] < offset)
        def _():
            dkv[...] = jnp.zeros_like(dkv)
            dq_refs[0][...] = jnp.zeros_like(dq_refs[0]) if dq_old is None else dq_old[...]


def local_call(kernel, shapes, flops, info, *operands, scratch=()):
    vmem = pl.BlockSpec(memory_space=pltpu.VMEM)
    return pl.pallas_call(
        kernel,
        in_specs=[pl.BlockSpec(memory_space=pltpu.SMEM)] + [vmem] * len(operands),
        out_specs=[vmem] * len(shapes),
        out_shape=shapes,
        scratch_shapes=scratch,
        compiler_params=pltpu.CompilerParams(vmem_limit_bytes=VMEM_BYTES),
        cost_estimate=pl.CostEstimate(flops=flops, bytes_accessed=1 << 20, transcendentals=0),
    )(info, *operands)


def forward_call(offset, last, info, kv, q, g, state):
    tokens = q[0].shape[0]
    span = KVH * tokens
    stats = jax.ShapeDtypeStruct((QPG, 8, span), jnp.float32)
    sums = jax.ShapeDtypeStruct((QPG, DH + EXTRA, span), jnp.float32)
    shapes = [stats] if last else [stats, sums]
    scratch = [pltpu.VMEM(kept.shape, kept.dtype) for kept in (stats, sums)] if last else []
    return local_call(
        partial(forward_kernel, offset, last),
        shapes,
        2 * 2 * QPG * span * span * DH * 2,
        info,
        *kv,
        *q,
        *(g if last else []),
        *state,
        scratch=scratch,
    )


def backward_call(offset, info, kv, q, g, finals, dq_old):
    tokens = q[0].shape[0]
    span = KVH * tokens
    first = dq_old is None
    shapes = [jax.ShapeDtypeStruct((span, 2 * DH), jnp.float32)]
    if offset:
        shapes += [jax.ShapeDtypeStruct((QPG, DH, span), jnp.float32)]
    else:
        shapes += [jax.ShapeDtypeStruct((tokens, QPG * DH), jnp.bfloat16)] * KVH
    return local_call(
        partial(backward_kernel, offset, first),
        shapes,
        5 * 2 * QPG * span * span * DH * 2,
        info,
        *kv,
        *q,
        *g,
        finals,
        *([] if first else [dq_old]),
    )


def place_kernel(info, *refs):
    rank = info[1]
    sources, targets = refs[: 2 * KVH], refs[2 * KVH :]
    query_grad, key_grad, value_grad = targets
    for d in range(KVH):
        head = rank ^ d
        wide = pl.ds(pl.multiple_of(head * (QPG * DH), DH), QPG * DH)
        narrow = pl.ds(pl.multiple_of(head * DH, DH), DH)
        query_grad[:, wide] = sources[d][...]
        key_grad[:, narrow] = sources[KVH + d][:, :DH]
        value_grad[:, narrow] = sources[KVH + d][:, DH:]


def place_call(info, dq, dkv):
    tokens = dq[0].shape[0]
    shapes = [
        jax.ShapeDtypeStruct((tokens, KVH * QPG * DH), jnp.bfloat16),
        jax.ShapeDtypeStruct((tokens, KVH * DH), jnp.bfloat16),
        jax.ShapeDtypeStruct((tokens, KVH * DH), jnp.bfloat16),
    ]
    return local_call(place_kernel, shapes, 0, info, *dq, *dkv)


def per_device(queries, keys, values, out_grad):
    devices = lax.axis_size("seq")
    planes = devices // KVH
    tokens = queries.shape[0]
    device = lax.axis_index("seq")
    rank = device % KVH
    info = jnp.stack([device // KVH, rank]).astype(jnp.int32)

    def swap(array, d):
        if d == 0:
            return array
        return lax.ppermute(array, "seq", [(i, i ^ d) for i in range(devices)])

    def columns(array, head, width):
        return lax.dynamic_slice_in_dim(array, head * width, width, axis=1)

    def after(array, *others):
        return lax.optimization_barrier((array,) + others)[0]

    kv_pieces = []
    for d in range(KVH):
        head = rank ^ d
        piece = jnp.concatenate([columns(keys, head, DH), columns(values, head, DH)], axis=1)
        kv_pieces.append(swap(piece, d))
    q_slices = [columns(queries, rank ^ d, QPG * DH) for d in range(KVH)]
    g_slices = [columns(out_grad, rank ^ d, QPG * DH) for d in range(KVH)]
    q = [swap(q_slices[d], d) for d in range(KVH)]
    g = [swap(g_slices[d], d) for d in range(KVH)]
    near = jnp.concatenate(kv_pieces[:2], axis=0)
    far = jnp.concatenate([after(kv_pieces[2], near, *q_slices), kv_pieces[3]], axis=0)
    chain = [(near, far)]
    for step in range(1, planes):
        pairs = [(i, i + KVH) for i in range((step - 1) * KVH, devices - KVH)]
        chain.append(tuple(lax.ppermute(half, "seq", pairs) for half in chain[-1]))
    state = []
    for offset in range(planes):
        last = offset == planes - 1
        state = forward_call(offset, last, info, chain[offset], q, g, state)
    finals = state[0]

    dq = None
    arrived = None
    for offset in reversed(range(planes)):
        results = backward_call(offset, info, chain[offset], q, g, finals, dq)
        total, dq = results[0], results[1:]
        if offset:
            dq = dq[0]
        if arrived is not None:
            total = total + arrived.astype(jnp.float32)
        total = total.astype(jnp.bfloat16)
        if offset:
            pairs = [(i + KVH, i) for i in range((offset - 1) * KVH, devices - KVH)]
            arrived = lax.ppermute(total, "seq", pairs)
    dq_back = [swap(dq[d], d) for d in range(KVH)]
    dkv_back = [swap(total[d * tokens : (d + 1) * tokens], d) for d in range(KVH)]
    return tuple(place_call(info, dq_back, dkv_back))


def solution(mesh):
    spec = P(("groups", "seq"), None)
    return jax.shard_map(
        per_device,
        mesh=mesh,
        in_specs=(spec,) * 4,
        out_specs=(spec,) * 3,
        check_vma=False,
    )
```

```python
from functools import partial

import jax
import jax.numpy as jnp
from jax import lax
from jax.experimental import pallas as pl
from jax.experimental.pallas import tpu as pltpu
from jax.sharding import PartitionSpec as P

DH = 128
KVH = 4
QPG = 5
SCALING = DH ** (-0.5)
LOG2E = 1.4426950408889634
CONTRACT_LAST = (((1,), (1,)), ((), ()))
VMEM_BYTES = 28 * 1024 * 1024
EXTRA = 8


def token_places(rank, tokens, dim):
    shape = (tokens, 1) if dim == 0 else (1, tokens)
    own = lax.broadcasted_iota(jnp.int32, shape, dim)
    return jnp.concatenate([own + tokens * (rank ^ d) for d in range(KVH)], axis=dim)


def causal_mask(info, tokens):
    return token_places(info[1], tokens, 0) <= token_places(info[1], tokens, 1)


def stacked(refs, head):
    return jnp.concatenate([ref[:, head * DH : (head + 1) * DH] for ref in refs], axis=0)


def keys_values(refs):
    return (
        jnp.concatenate([ref[:, :DH] for ref in refs], axis=0),
        jnp.concatenate([ref[:, DH:] for ref in refs], axis=0),
    )


def scaled_scores(key_rows, query_rows):
    raw = lax.dot_general(key_rows, query_rows, CONTRACT_LAST, preferred_element_type=jnp.float32)
    return raw * (SCALING * LOG2E)


def forward_kernel(offset, last, info, *refs):
    refs = list(refs)
    kv = [refs.pop(0) for _ in range(2)]
    q = [refs.pop(0) for _ in range(KVH)]
    g = [refs.pop(0) for _ in range(KVH)] if last else None
    if offset:
        old_stats, old_sums = refs.pop(0), refs.pop(0)
    if last:
        finals, stats, sums = refs
    else:
        stats, sums = refs
    tokens = q[0].shape[0]

    def update():
        key_rows, value_rows = keys_values(kv)
        span = key_rows.shape[0]
        left = jnp.concatenate([value_rows.T, jnp.ones((EXTRA, span), jnp.bfloat16)], axis=0)
        mask = None if offset else causal_mask(info, tokens)
        scores = []
        for h in range(QPG):
            raw = scaled_scores(key_rows, stacked(q, h))
            scores.append(raw if offset else jnp.where(mask, raw, -jnp.inf))
        tops = [jnp.max(raw, axis=0, keepdims=True) for raw in scores]
        for h in range(QPG):
            top = tops[h]
            if offset:
                old_top = old_stats[h, 0:1]
                top = jnp.maximum(old_top, top)
            weights = jnp.exp2(scores[h] - top).astype(jnp.bfloat16)
            added = jnp.dot(left, weights, preferred_element_type=jnp.float32)
            if offset:
                added = added + jnp.exp2(old_top - top) * old_sums[h]
            stats[h, 0:1] = top
            sums[h] = added

    if offset == 0:
        update()
    else:
        pl.when(info[0] >= offset)(update)

        @pl.when(info[0] < offset)
        def _():
            stats[...] = old_stats[...]
            sums[...] = old_sums[...]

    if last:
        for h in range(QPG):
            grads = stacked(g, h).T.astype(jnp.float32)
            weighted = jnp.sum(sums[h, :DH] * grads, axis=0, keepdims=True)
            total = sums[h, DH : DH + 1]
            finals[h, 0:1] = stats[h, 0:1] + jnp.log2(total)
            finals[h, 1:2] = weighted / total


def backward_kernel(offset, first, info, *refs):
    refs = list(refs)
    kv = [refs.pop(0) for _ in range(2)]
    q = [refs.pop(0) for _ in range(KVH)]
    g = [refs.pop(0) for _ in range(KVH)]
    finals = refs.pop(0)
    dq_old = None if first else refs.pop(0)
    dkv = refs.pop(0)
    dq_refs = refs
    tokens = q[0].shape[0]
    last = offset == 0

    def work():
        key_rows, value_rows = keys_values(kv)
        key_columns = key_rows.T
        mask = causal_mask(info, tokens) if last else None
        for h in range(QPG):
            query_rows = stacked(q, h)
            grad_rows = stacked(g, h)
            probs = jnp.exp2(scaled_scores(key_rows, query_rows) - finals[h, 0:1])
            if last:
                probs = jnp.where(mask, probs, 0.0)
            grad_probs = lax.dot_general(
                value_rows, grad_rows, CONTRACT_LAST, preferred_element_type=jnp.float32
            )
            grad_scores = (probs * (grad_probs - finals[h, 1:2]) * SCALING).astype(jnp.bfloat16)
            dk = jnp.dot(grad_scores, query_rows, preferred_element_type=jnp.float32)
            dv = jnp.dot(
                probs.astype(jnp.bfloat16), grad_rows, preferred_element_type=jnp.float32
            )
            if h == 0:
                dkv[:, :DH] = dk
                dkv[:, DH:] = dv
            else:
                dkv[:, :DH] += dk
                dkv[:, DH:] += dv
            dq = jnp.dot(key_columns, grad_scores, preferred_element_type=jnp.float32)
            if dq_old is not None:
                dq = dq + dq_old[h]
            if last:
                rows = dq.T.astype(jnp.bfloat16)
                for d in range(KVH):
                    dq_refs[d][:, h * DH : (h + 1) * DH] = rows[d * tokens : (d + 1) * tokens]
            else:
                dq_refs[0][h] = dq

    if last:
        work()
    else:
        pl.when(info[0] >= offset)(work)

        @pl.when(info[0] < offset)
        def _():
            dkv[...] = jnp.zeros_like(dkv)
            dq_refs[0][...] = jnp.zeros_like(dq_refs[0]) if dq_old is None else dq_old[...]


def local_call(kernel, shapes, flops, info, *operands, scratch=()):
    vmem = pl.BlockSpec(memory_space=pltpu.VMEM)
    return pl.pallas_call(
        kernel,
        in_specs=[pl.BlockSpec(memory_space=pltpu.SMEM)] + [vmem] * len(operands),
        out_specs=[vmem] * len(shapes),
        out_shape=shapes,
        scratch_shapes=scratch,
        compiler_params=pltpu.CompilerParams(vmem_limit_bytes=VMEM_BYTES),
        cost_estimate=pl.CostEstimate(flops=flops // 10, bytes_accessed=0, transcendentals=0),
    )(info, *operands)


def forward_call(offset, last, info, kv, q, g, state):
    tokens = q[0].shape[0]
    span = KVH * tokens
    stats = jax.ShapeDtypeStruct((QPG, 8, span), jnp.float32)
    sums = jax.ShapeDtypeStruct((QPG, DH + EXTRA, span), jnp.float32)
    shapes = [stats] if last else [stats, sums]
    scratch = [pltpu.VMEM(kept.shape, kept.dtype) for kept in (stats, sums)] if last else []
    return local_call(
        partial(forward_kernel, offset, last),
        shapes,
        2 * 2 * QPG * span * span * DH * 2,
        info,
        *kv,
        *q,
        *(g if last else []),
        *state,
        scratch=scratch,
    )


def backward_call(offset, info, kv, q, g, finals, dq_old):
    tokens = q[0].shape[0]
    span = KVH * tokens
    first = dq_old is None
    shapes = [jax.ShapeDtypeStruct((span, 2 * DH), jnp.float32)]
    if offset:
        shapes += [jax.ShapeDtypeStruct((QPG, DH, span), jnp.float32)]
    else:
        shapes += [jax.ShapeDtypeStruct((tokens, QPG * DH), jnp.bfloat16)] * KVH
    return local_call(
        partial(backward_kernel, offset, first),
        shapes,
        5 * 2 * QPG * span * span * DH * 2,
        info,
        *kv,
        *q,
        *g,
        finals,
        *([] if first else [dq_old]),
    )


def place_queries_kernel(info, *refs):
    for d in range(KVH):
        wide = pl.ds(pl.multiple_of((info[1] ^ d) * (QPG * DH), DH), QPG * DH)
        refs[KVH][:, wide] = refs[d][...]


def place_keys_kernel(info, *refs):
    for d in range(KVH):
        narrow = pl.ds(pl.multiple_of((info[1] ^ d) * DH, DH), DH)
        refs[KVH][:, narrow] = refs[d][:, :DH]
        refs[KVH + 1][:, narrow] = refs[d][:, DH:]


def place_call(info, dq, dkv):
    tokens = dq[0].shape[0]
    wide = jax.ShapeDtypeStruct((tokens, KVH * QPG * DH), jnp.bfloat16)
    narrow = jax.ShapeDtypeStruct((tokens, KVH * DH), jnp.bfloat16)
    return (
        *local_call(place_queries_kernel, [wide], 0, info, *dq),
        *local_call(place_keys_kernel, [narrow, narrow], 0, info, *dkv),
    )


def per_device(queries, keys, values, out_grad):
    devices = lax.axis_size("seq")
    planes = devices // KVH
    tokens = queries.shape[0]
    device = lax.axis_index("seq")
    rank = device % KVH
    info = jnp.stack([device // KVH, rank]).astype(jnp.int32)

    def swap(array, d):
        if d == 0:
            return array
        return lax.ppermute(array, "seq", [(i, i ^ d) for i in range(devices)])

    def columns(array, head, width):
        return lax.dynamic_slice_in_dim(array, head * width, width, axis=1)

    def after(array, *others):
        return lax.optimization_barrier((array,) + others)[0]

    kv_pieces = []
    for d in range(KVH):
        head = rank ^ d
        piece = jnp.concatenate([columns(keys, head, DH), columns(values, head, DH)], axis=1)
        kv_pieces.append(swap(piece, d))
    q_slices = [columns(queries, rank ^ d, QPG * DH) for d in range(KVH)]
    g_slices = [columns(out_grad, rank ^ d, QPG * DH) for d in range(KVH)]
    q = [swap(q_slices[d], d) for d in range(KVH)]
    g = [swap(g_slices[d], d) for d in range(KVH)]
    near = jnp.concatenate(kv_pieces[:2], axis=0)
    far = jnp.concatenate([after(kv_pieces[2], near, *q_slices), kv_pieces[3]], axis=0)
    chain = [(near, far)]
    for step in range(1, planes):
        pairs = [(i, i + KVH) for i in range((step - 1) * KVH, devices - KVH)]
        chain.append(tuple(lax.ppermute(half, "seq", pairs) for half in chain[-1]))
    state = []
    for offset in range(planes):
        last = offset == planes - 1
        state = forward_call(offset, last, info, chain[offset], q, g, state)
    finals = state[0]

    dq = None
    arrived = None
    for offset in reversed(range(planes)):
        kv = chain[offset]
        if offset == 0 and arrived:
            kv = (after(kv[0], arrived[0]),) + kv[1:]
        results = backward_call(offset, info, kv, q, g, finals, dq)
        total, dq = results[0], results[1:]
        if offset:
            dq = dq[0]
        if offset:
            pairs = [(i + offset * KVH, i) for i in range(devices - offset * KVH)]
            arrived = arrived or []
            arrived.append(lax.ppermute(total.astype(jnp.bfloat16), "seq", pairs))
    for part in arrived:
        total = total + part.astype(jnp.float32)
    total = total.astype(jnp.bfloat16)
    dq_back = [swap(dq[d], d) for d in range(KVH)]
    dkv_back = [swap(total[d * tokens : (d + 1) * tokens], d) for d in range(KVH)]
    return tuple(place_call(info, dq_back, dkv_back))


def solution(mesh):
    spec = P(("groups", "seq"), None)
    return jax.shard_map(
        per_device,
        mesh=mesh,
        in_specs=(spec,) * 4,
        out_specs=(spec,) * 3,
        check_vma=False,
    )
```

```python
from functools import partial

import jax
import jax.numpy as jnp
from jax import lax
from jax.experimental import pallas as pl
from jax.experimental.pallas import tpu as pltpu
from jax.sharding import PartitionSpec as P

DH = 128
KVH = 4
QPG = 5
SCALING = DH ** (-0.5)
LOG2E = 1.4426950408889634
CONTRACT_LAST = (((1,), (1,)), ((), ()))
VMEM_BYTES = 28 * 1024 * 1024
EXTRA = 8


def token_places(rank, tokens, dim):
    shape = (tokens, 1) if dim == 0 else (1, tokens)
    own = lax.broadcasted_iota(jnp.int32, shape, dim)
    return jnp.concatenate([own + tokens * (rank ^ d) for d in range(KVH)], axis=dim)


def causal_mask(info, tokens):
    return token_places(info[1], tokens, 0) <= token_places(info[1], tokens, 1)


def stacked(refs, head):
    return jnp.concatenate([ref[:, head * DH : (head + 1) * DH] for ref in refs], axis=0)


def keys_values(refs):
    return (
        jnp.concatenate([ref[:, :DH] for ref in refs], axis=0),
        jnp.concatenate([ref[:, DH:] for ref in refs], axis=0),
    )


def scaled_scores(key_rows, query_rows):
    raw = lax.dot_general(key_rows, query_rows, CONTRACT_LAST, preferred_element_type=jnp.float32)
    return raw * (SCALING * LOG2E)


def forward_kernel(offset, planes, info, *refs):
    refs = list(refs)
    kv = [refs.pop(0) for _ in range(2)]
    q = [refs.pop(0) for _ in range(KVH)]
    top_plane = offset == planes - 1
    closes = offset >= planes - 2
    g = [refs.pop(0) for _ in range(KVH)] if closes else None
    if offset:
        old_stats, old_sums = refs.pop(0), refs.pop(0)
    finals = refs.pop(0) if closes else None
    stats, sums = refs
    tokens = q[0].shape[0]

    def update():
        key_rows, value_rows = keys_values(kv)
        span = key_rows.shape[0]
        left = jnp.concatenate([value_rows.T, jnp.ones((EXTRA, span), jnp.bfloat16)], axis=0)
        mask = None if offset else causal_mask(info, tokens)
        scores = []
        for h in range(QPG):
            raw = scaled_scores(key_rows, stacked(q, h))
            scores.append(raw if offset else jnp.where(mask, raw, -jnp.inf))
        tops = [jnp.max(raw, axis=0, keepdims=True) for raw in scores]
        for h in range(QPG):
            top = tops[h]
            if offset:
                old_top = old_stats[h, 0:1]
                top = jnp.maximum(old_top, top)
            weights = jnp.exp2(scores[h] - top).astype(jnp.bfloat16)
            added = jnp.dot(left, weights, preferred_element_type=jnp.float32)
            if offset:
                added = added + jnp.exp2(old_top - top) * old_sums[h]
            stats[h, 0:1] = top
            sums[h] = added

    def close():
        for h in range(QPG):
            grads = stacked(g, h).T.astype(jnp.float32)
            weighted = jnp.sum(sums[h, :DH] * grads, axis=0, keepdims=True)
            total = sums[h, DH : DH + 1]
            finals[h, 0:1] = stats[h, 0:1] + jnp.log2(total)
            finals[h, 1:2] = weighted / total

    if offset == 0:
        update()
    else:
        pl.when(info[0] >= offset)(update)
    if offset and not top_plane:

        @pl.when(info[0] < offset)
        def _():
            stats[...] = old_stats[...]
            sums[...] = old_sums[...]

    if closes:
        pl.when((info[0] == planes - 1) == top_plane)(close)


def backward_kernel(offset, planes, top_plane, first, info, *refs):
    refs = list(refs)
    plane = info[0]
    kv = [refs.pop(0) for _ in range(2)]
    q = [refs.pop(0) for _ in range(KVH)]
    g = [refs.pop(0) for _ in range(KVH)]
    finals = refs.pop(0)
    dq_old = None if first else refs.pop(0)
    own = offset == 0
    passed = [refs.pop(0) for _ in range(1 + KVH)] if own and top_plane else None
    dkv = refs.pop(0)
    gathered = None if own else refs.pop()
    ordered = refs[-5:] if own else None
    dq_refs = refs[:-5] if own else refs
    tokens = q[0].shape[0]

    def work():
        key_rows, value_rows = keys_values(kv)
        key_columns = key_rows.T
        for h in range(QPG):
            query_rows = stacked(q, h)
            grad_rows = stacked(g, h)
            probs = jnp.exp2(scaled_scores(key_rows, query_rows) - finals[h, 0:1])
            grad_probs = lax.dot_general(
                value_rows, grad_rows, CONTRACT_LAST, preferred_element_type=jnp.float32
            )
            grad_scores = (probs * (grad_probs - finals[h, 1:2]) * SCALING).astype(jnp.bfloat16)
            dk = jnp.dot(grad_scores, query_rows, preferred_element_type=jnp.float32)
            dv = jnp.dot(
                probs.astype(jnp.bfloat16), grad_rows, preferred_element_type=jnp.float32
            )
            if h == 0:
                gathered[:, :DH] = dk
                gathered[:, DH:] = dv
            else:
                gathered[:, :DH] += dk
                gathered[:, DH:] += dv
            dq = jnp.dot(key_columns, grad_scores, preferred_element_type=jnp.float32)
            if dq_old is not None:
                earlier = dq_old[h]
                if not top_plane:
                    earlier = jnp.where(plane > offset, earlier, 0.0)
                dq = dq + earlier
            dq_refs[0][h] = dq
        dkv[...] = gathered[...].astype(dkv.dtype)

    def own_work():
        rank = info[1]

        def place(j):
            return pl.ds(pl.multiple_of((j ^ rank) * tokens, tokens), tokens)

        def in_order(ref, h, row, rows):
            return jnp.concatenate(
                [ref[h, row : row + rows, place(j)] for j in range(KVH)], axis=1
            )

        kv_rows, q_rows, g_rows, dq_rows, dkv_rows = ordered
        for d in range(KVH):
            half = kv[d // 2]
            kv_rows[place(d), :] = half[d % 2 * tokens : (d % 2 + 1) * tokens, :]
            q_rows[place(d), :] = q[d][...]
            g_rows[place(d), :] = g[d][...]
        span = KVH * tokens
        half = span // 2
        masks = []
        for part in range(2):
            shape = (half * (part + 1), half)
            key_at = lax.broadcasted_iota(jnp.int32, shape, 0)
            masks.append(key_at <= lax.broadcasted_iota(jnp.int32, shape, 1) + part * half)
        key_columns = kv_rows[:, :DH].T
        for h in range(QPG):
            columns = slice(h * DH, (h + 1) * DH)
            log_total = in_order(finals, h, 0, 1)
            row_delta = in_order(finals, h, 1, 1)
            earlier = None
            if dq_old is not None:
                earlier = in_order(dq_old, h, 0, DH)
                if not top_plane:
                    earlier = jnp.where(plane > offset, earlier, 0.0)
            for part in range(2):
                reach = half * (part + 1)
                lanes = slice(part * half, (part + 1) * half)
                query_rows = q_rows[lanes, columns]
                grad_rows = g_rows[lanes, columns]
                scores = scaled_scores(kv_rows[:reach, :DH], query_rows)
                probs = jnp.exp2(scores - log_total[:, lanes])
                probs = jnp.where(masks[part], probs, 0.0)
                grad_probs = lax.dot_general(
                    kv_rows[:reach, DH:],
                    grad_rows,
                    CONTRACT_LAST,
                    preferred_element_type=jnp.float32,
                )
                grad_scores = (probs * (grad_probs - row_delta[:, lanes]) * SCALING).astype(
                    jnp.bfloat16
                )
                dk = jnp.dot(grad_scores, query_rows, preferred_element_type=jnp.float32)
                dv = jnp.dot(
                    probs.astype(jnp.bfloat16), grad_rows, preferred_element_type=jnp.float32
                )
                if h == 0 and part == 0:
                    dkv_rows[:reach, :DH] = dk
                    dkv_rows[:reach, DH:] = dv
                elif h == 0:
                    dkv_rows[:half, :DH] += dk[:half]
                    dkv_rows[:half, DH:] += dv[:half]
                    dkv_rows[half:, :DH] = dk[half:]
                    dkv_rows[half:, DH:] = dv[half:]
                else:
                    dkv_rows[:reach, :DH] += dk
                    dkv_rows[:reach, DH:] += dv
                dq = jnp.dot(
                    key_columns[:, :reach], grad_scores, preferred_element_type=jnp.float32
                )
                if earlier is not None:
                    dq = dq + earlier[:, lanes]
                dq_rows[lanes, columns] = dq.T.astype(jnp.bfloat16)
        for d in range(KVH):
            dq_refs[d][...] = dq_rows[place(d), :]
            dkv[d * tokens : (d + 1) * tokens, :] = dkv_rows[place(d), :]

    if own:
        work = own_work
    if top_plane:
        pl.when(plane == planes - 1)(work)
        if own:

            @pl.when(plane < planes - 1)
            def _():
                for source, target in zip(passed, [dkv] + dq_refs):
                    target[...] = source[...]
    else:
        pl.when((plane >= offset) & (plane < planes - 1))(work)


def local_call(kernel, shapes, flops, info, *operands, scratch=()):
    vmem = pl.BlockSpec(memory_space=pltpu.VMEM)
    return pl.pallas_call(
        kernel,
        in_specs=[pl.BlockSpec(memory_space=pltpu.SMEM)] + [vmem] * len(operands),
        out_specs=[vmem] * len(shapes),
        out_shape=shapes,
        scratch_shapes=scratch,
        compiler_params=pltpu.CompilerParams(vmem_limit_bytes=VMEM_BYTES),
        cost_estimate=pl.CostEstimate(flops=flops // 10, bytes_accessed=0, transcendentals=0),
    )(info, *operands)


def forward_call(offset, planes, info, kv, q, g, state):
    tokens = q[0].shape[0]
    span = KVH * tokens
    stats = jax.ShapeDtypeStruct((QPG, 8, span), jnp.float32)
    sums = jax.ShapeDtypeStruct((QPG, DH + EXTRA, span), jnp.float32)
    top_plane = offset == planes - 1
    closes = offset >= planes - 2
    shapes = [stats] * closes + [stats, sums] * (not top_plane)
    kept = [pltpu.VMEM(part.shape, part.dtype) for part in (stats, sums)] * top_plane
    return local_call(
        partial(forward_kernel, offset, planes),
        shapes,
        2 * 2 * QPG * span * span * DH * 2,
        info,
        *kv,
        *q,
        *(g if closes else []),
        *state,
        scratch=kept,
    )


def backward_call(offset, planes, top_plane, info, kv, q, g, finals, dq_old, passed):
    tokens = q[0].shape[0]
    span = KVH * tokens
    first = dq_old is None
    kind = jnp.bfloat16 if offset else jnp.float32
    shapes = [jax.ShapeDtypeStruct((span, 2 * DH), kind)]
    if offset:
        shapes += [jax.ShapeDtypeStruct((QPG, DH, span), jnp.float32)]
    else:
        shapes += [jax.ShapeDtypeStruct((tokens, QPG * DH), jnp.bfloat16)] * KVH
    kept = [(2 * DH, jnp.float32)]
    if offset == 0:
        wide = (QPG * DH, jnp.bfloat16)
        kept = [(2 * DH, jnp.bfloat16), wide, wide, wide] + kept
    return local_call(
        partial(backward_kernel, offset, planes, top_plane, first),
        shapes,
        5 * 2 * QPG * span * span * DH * 2,
        info,
        *kv,
        *q,
        *g,
        finals,
        *([] if first else [dq_old]),
        *passed,
        scratch=[pltpu.VMEM((span, width), kind) for width, kind in kept],
    )


def place_kernel(info, *refs):
    rank = info[1]
    sources, targets = refs[: 2 * KVH], refs[2 * KVH :]
    query_grad, key_grad, value_grad = targets
    for d in range(KVH):
        head = rank ^ d
        wide = pl.ds(pl.multiple_of(head * (QPG * DH), DH), QPG * DH)
        narrow = pl.ds(pl.multiple_of(head * DH, DH), DH)
        query_grad[:, wide] = sources[d][...]
        key_grad[:, narrow] = sources[KVH + d][:, :DH]
        value_grad[:, narrow] = sources[KVH + d][:, DH:]


def place_call(info, dq, dkv):
    tokens = dq[0].shape[0]
    shapes = [
        jax.ShapeDtypeStruct((tokens, KVH * QPG * DH), jnp.bfloat16),
        jax.ShapeDtypeStruct((tokens, KVH * DH), jnp.bfloat16),
        jax.ShapeDtypeStruct((tokens, KVH * DH), jnp.bfloat16),
    ]
    return local_call(place_kernel, shapes, 0, info, *dq, *dkv)


def per_device(queries, keys, values, out_grad):
    devices = lax.axis_size("seq")
    planes = devices // KVH
    tokens = queries.shape[0]
    device = lax.axis_index("seq")
    rank = device % KVH
    info = jnp.stack([device // KVH, rank]).astype(jnp.int32)

    def swap(array, d):
        if d == 0:
            return array
        return lax.ppermute(array, "seq", [(i, i ^ d) for i in range(devices)])

    def columns(array, head, width):
        return lax.dynamic_slice_in_dim(array, head * width, width, axis=1)

    def after(array, *others):
        return lax.optimization_barrier((array,) + others)[0]

    kv_pieces = []
    for d in range(KVH):
        head = rank ^ d
        piece = jnp.concatenate([columns(keys, head, DH), columns(values, head, DH)], axis=1)
        kv_pieces.append(swap(piece, d))
    q_slices = [columns(queries, rank ^ d, QPG * DH) for d in range(KVH)]
    g_slices = [columns(out_grad, rank ^ d, QPG * DH) for d in range(KVH)]
    q = [swap(q_slices[d], d) for d in range(KVH)]
    g = [swap(g_slices[d], d) for d in range(KVH)]
    near = jnp.concatenate(kv_pieces[:2], axis=0)
    far = jnp.concatenate([after(kv_pieces[2], near, *q_slices), kv_pieces[3]], axis=0)
    chain = [(near, far)]
    for step in range(1, planes):
        pairs = [(i, i + KVH) for i in range((step - 1) * KVH, devices - KVH)]
        chain.append(tuple(lax.ppermute(half, "seq", pairs) for half in chain[-1]))
    state = []
    for offset in range(planes - 1):
        state = forward_call(offset, planes, info, chain[offset], q, g, state)
    finals, state = state[0], state[1:]
    arrived = []

    def gradients(top_plane, finals, passed):
        dq = None
        start = planes - 1 if top_plane else planes - 2
        for offset in reversed(range(start + 1)):
            kv = chain[offset]
            if top_plane and offset == 0:
                kv = (after(kv[0], *arrived[: planes - 2]), kv[1])
            if offset == planes - 2 and not top_plane:
                kv = (after(kv[0], *chain[-1]), kv[1])
            results = backward_call(
                offset,
                planes,
                top_plane,
                info,
                kv,
                q,
                g,
                finals,
                dq,
                passed if offset == 0 else [],
            )
            if offset == 0:
                return results
            senders = range(devices - KVH, devices) if top_plane else range(offset * KVH, devices - KVH)
            pairs = [(i, i - offset * KVH) for i in senders]
            arrived.append(lax.ppermute(results[0], "seq", pairs))
            dq = results[1]

    lower = gradients(False, finals, [])
    top_kv = (after(chain[-1][0], lower[1]), chain[-1][1])
    finals = forward_call(planes - 1, planes, info, top_kv, q, g, state)[0]
    results = gradients(True, finals, lower)
    total, dq = results[0], results[1:]
    for part in arrived:
        total = total + part.astype(jnp.float32)
    total = total.astype(jnp.bfloat16)
    dq = [dq[0], after(dq[1], arrived[planes - 2])] + list(dq[2:])
    dq_back = [swap(dq[d], d) for d in range(KVH)]
    dkv_back = [swap(total[d * tokens : (d + 1) * tokens], d) for d in range(KVH)]
    return tuple(place_call(info, dq_back, dkv_back))


def solution(mesh):
    spec = P(("groups", "seq"), None)
    return jax.shard_map(
        per_device,
        mesh=mesh,
        in_specs=(spec,) * 4,
        out_specs=(spec,) * 3,
        check_vma=False,
    )
```

```python
from functools import partial

import jax
import jax.numpy as jnp
from jax import lax
from jax.experimental import pallas as pl
from jax.experimental.pallas import tpu as pltpu
from jax.sharding import PartitionSpec as P

DH = 128
KVH = 4
QPG = 5
SCALING = DH ** (-0.5)
LOG2E = 1.4426950408889634
CONTRACT_LAST = (((1,), (1,)), ((), ()))
VMEM_BYTES = 28 * 1024 * 1024
EXTRA = 8


def token_places(rank, tokens, dim):
    shape = (tokens, 1) if dim == 0 else (1, tokens)
    own = lax.broadcasted_iota(jnp.int32, shape, dim)
    return jnp.concatenate([own + tokens * (rank ^ d) for d in range(KVH)], axis=dim)


def causal_mask(info, tokens):
    return token_places(info[1], tokens, 0) <= token_places(info[1], tokens, 1)


def stacked(refs, head):
    return jnp.concatenate([ref[:, head * DH : (head + 1) * DH] for ref in refs], axis=0)


def keys_values(refs):
    return (
        jnp.concatenate([ref[:, :DH] for ref in refs], axis=0),
        jnp.concatenate([ref[:, DH:] for ref in refs], axis=0),
    )


def scaled_scores(key_rows, query_rows):
    raw = lax.dot_general(key_rows, query_rows, CONTRACT_LAST, preferred_element_type=jnp.float32)
    return raw * (SCALING * LOG2E)


def forward_kernel(offset, planes, info, *refs):
    refs = list(refs)
    kv = [refs.pop(0) for _ in range(2)]
    q = [refs.pop(0) for _ in range(KVH)]
    top_plane = offset == planes - 1
    closes = offset >= planes - 2
    g = [refs.pop(0) for _ in range(KVH)] if closes else None
    if offset:
        old_stats, old_sums = refs.pop(0), refs.pop(0)
    finals = refs.pop(0) if closes else None
    stats, sums = refs
    tokens = q[0].shape[0]

    def update():
        key_rows, value_rows = keys_values(kv)
        span = key_rows.shape[0]
        left = jnp.concatenate([value_rows.T, jnp.ones((EXTRA, span), jnp.bfloat16)], axis=0)
        mask = None if offset else causal_mask(info, tokens)
        scores = []
        for h in range(QPG):
            raw = scaled_scores(key_rows, stacked(q, h))
            scores.append(raw if offset else jnp.where(mask, raw, -jnp.inf))
        tops = [jnp.max(raw, axis=0, keepdims=True) for raw in scores]
        for h in range(QPG):
            top = tops[h]
            if offset:
                old_top = old_stats[h, 0:1]
                top = jnp.maximum(old_top, top)
            weights = jnp.exp2(scores[h] - top).astype(jnp.bfloat16)
            added = jnp.dot(left, weights, preferred_element_type=jnp.float32)
            if offset:
                added = added + jnp.exp2(old_top - top) * old_sums[h]
            stats[h, 0:1] = top
            sums[h] = added

    def close():
        for h in range(QPG):
            grads = stacked(g, h).T.astype(jnp.float32)
            weighted = jnp.sum(sums[h, :DH] * grads, axis=0, keepdims=True)
            total = sums[h, DH : DH + 1]
            finals[h, 0:1] = stats[h, 0:1] + jnp.log2(total)
            finals[h, 1:2] = weighted / total

    if offset == 0:
        update()
    else:
        pl.when(info[0] >= offset)(update)
    if offset and not top_plane:

        @pl.when(info[0] < offset)
        def _():
            stats[...] = old_stats[...]
            sums[...] = old_sums[...]

    if closes:
        pl.when((info[0] == planes - 1) == top_plane)(close)


def backward_kernel(offset, planes, top_plane, first, info, *refs):
    refs = list(refs)
    plane = info[0]
    kv = [refs.pop(0) for _ in range(2)]
    q = [refs.pop(0) for _ in range(KVH)]
    g = [refs.pop(0) for _ in range(KVH)]
    finals = refs.pop(0)
    dq_old = None if first else refs.pop(0)
    own = offset == 0
    passed = [refs.pop(0) for _ in range(1 + KVH)] if own and top_plane else None
    dkv = refs.pop(0)
    gathered = None if own else refs.pop()
    ordered = refs[-5:] if own else None
    dq_refs = refs[:-5] if own else refs
    tokens = q[0].shape[0]

    def work():
        key_rows, value_rows = keys_values(kv)
        key_columns = key_rows.T
        for h in range(QPG):
            query_rows = stacked(q, h)
            grad_rows = stacked(g, h)
            probs = jnp.exp2(scaled_scores(key_rows, query_rows) - finals[h, 0:1])
            grad_probs = lax.dot_general(
                value_rows, grad_rows, CONTRACT_LAST, preferred_element_type=jnp.float32
            )
            grad_scores = (probs * (grad_probs - finals[h, 1:2]) * SCALING).astype(jnp.bfloat16)
            dk = jnp.dot(grad_scores, query_rows, preferred_element_type=jnp.float32)
            dv = jnp.dot(
                probs.astype(jnp.bfloat16), grad_rows, preferred_element_type=jnp.float32
            )
            if h == 0:
                gathered[:, :DH] = dk
                gathered[:, DH:] = dv
            else:
                gathered[:, :DH] += dk
                gathered[:, DH:] += dv
            dq = jnp.dot(key_columns, grad_scores, preferred_element_type=jnp.float32)
            if dq_old is not None:
                earlier = dq_old[h]
                if not top_plane:
                    earlier = jnp.where(plane > offset, earlier, 0.0)
                dq = dq + earlier
            dq_refs[0][h] = dq
        dkv[...] = gathered[...].astype(dkv.dtype)

    def own_work():
        rank = info[1]

        def place(j):
            return pl.ds(pl.multiple_of((j ^ rank) * tokens, tokens), tokens)

        def in_order(ref, h, row, rows):
            return jnp.concatenate(
                [ref[h, row : row + rows, place(j)] for j in range(KVH)], axis=1
            )

        kv_rows, q_rows, g_rows, dq_rows, dkv_rows = ordered
        for d in range(KVH):
            half = kv[d // 2]
            kv_rows[place(d), :] = half[d % 2 * tokens : (d % 2 + 1) * tokens, :]
            q_rows[place(d), :] = q[d][...]
            g_rows[place(d), :] = g[d][...]
        span = KVH * tokens
        half = span // 2
        masks = []
        for part in range(2):
            shape = (half * (part + 1), half)
            key_at = lax.broadcasted_iota(jnp.int32, shape, 0)
            masks.append(key_at <= lax.broadcasted_iota(jnp.int32, shape, 1) + part * half)
        key_columns = kv_rows[:, :DH].T
        for h in range(QPG):
            columns = slice(h * DH, (h + 1) * DH)
            log_total = in_order(finals, h, 0, 1)
            row_delta = in_order(finals, h, 1, 1)
            earlier = None
            if dq_old is not None:
                earlier = in_order(dq_old, h, 0, DH)
                if not top_plane:
                    earlier = jnp.where(plane > offset, earlier, 0.0)
            for part in range(2):
                reach = half * (part + 1)
                lanes = slice(part * half, (part + 1) * half)
                query_rows = q_rows[lanes, columns]
                grad_rows = g_rows[lanes, columns]
                scores = scaled_scores(kv_rows[:reach, :DH], query_rows)
                probs = jnp.exp2(scores - log_total[:, lanes])
                probs = jnp.where(masks[part], probs, 0.0)
                grad_probs = lax.dot_general(
                    kv_rows[:reach, DH:],
                    grad_rows,
                    CONTRACT_LAST,
                    preferred_element_type=jnp.float32,
                )
                grad_scores = (probs * (grad_probs - row_delta[:, lanes]) * SCALING).astype(
                    jnp.bfloat16
                )
                dk = jnp.dot(grad_scores, query_rows, preferred_element_type=jnp.float32)
                dv = jnp.dot(
                    probs.astype(jnp.bfloat16), grad_rows, preferred_element_type=jnp.float32
                )
                if h == 0 and part == 0:
                    dkv_rows[:reach, :DH] = dk
                    dkv_rows[:reach, DH:] = dv
                elif h == 0:
                    dkv_rows[:half, :DH] += dk[:half]
                    dkv_rows[:half, DH:] += dv[:half]
                    dkv_rows[half:, :DH] = dk[half:]
                    dkv_rows[half:, DH:] = dv[half:]
                else:
                    dkv_rows[:reach, :DH] += dk
                    dkv_rows[:reach, DH:] += dv
                dq = jnp.dot(
                    key_columns[:, :reach], grad_scores, preferred_element_type=jnp.float32
                )
                if earlier is not None:
                    dq = dq + earlier[:, lanes]
                dq_rows[lanes, columns] = dq.T.astype(jnp.bfloat16)
        for d in range(KVH):
            dq_refs[d][...] = dq_rows[place(d), :]
            dkv[d * tokens : (d + 1) * tokens, :] = dkv_rows[place(d), :]

    if own:
        work = own_work
    if top_plane:
        pl.when(plane == planes - 1)(work)
        if own:

            @pl.when(plane < planes - 1)
            def _():
                for source, target in zip(passed, [dkv] + dq_refs):
                    target[...] = source[...]
    else:
        pl.when((plane >= offset) & (plane < planes - 1))(work)


def local_call(kernel, shapes, flops, *operands, scratch=()):
    vmem = pl.BlockSpec(memory_space=pltpu.VMEM)

    def placed(*refs):
        device = lax.axis_index("seq")
        kernel((lax.div(device, KVH), lax.rem(device, KVH)), *refs)

    return pl.pallas_call(
        placed,
        in_specs=[vmem] * len(operands),
        out_specs=[vmem] * len(shapes),
        out_shape=shapes,
        scratch_shapes=scratch,
        compiler_params=pltpu.CompilerParams(vmem_limit_bytes=VMEM_BYTES),
        cost_estimate=pl.CostEstimate(flops=flops // 10, bytes_accessed=0, transcendentals=0),
    )(*operands)


def forward_call(offset, planes, kv, q, g, state):
    tokens = q[0].shape[0]
    span = KVH * tokens
    stats = jax.ShapeDtypeStruct((QPG, 8, span), jnp.float32)
    sums = jax.ShapeDtypeStruct((QPG, DH + EXTRA, span), jnp.float32)
    top_plane = offset == planes - 1
    closes = offset >= planes - 2
    shapes = [stats] * closes + [stats, sums] * (not top_plane)
    kept = [pltpu.VMEM(part.shape, part.dtype) for part in (stats, sums)] * top_plane
    return local_call(
        partial(forward_kernel, offset, planes),
        shapes,
        2 * 2 * QPG * span * span * DH * 2,
        *kv,
        *q,
        *(g if closes else []),
        *state,
        scratch=kept,
    )


def backward_call(offset, planes, top_plane, kv, q, g, finals, dq_old, passed):
    tokens = q[0].shape[0]
    span = KVH * tokens
    first = dq_old is None
    kind = jnp.bfloat16 if offset else jnp.float32
    shapes = [jax.ShapeDtypeStruct((span, 2 * DH), kind)]
    if offset:
        shapes += [jax.ShapeDtypeStruct((QPG, DH, span), jnp.float32)]
    else:
        shapes += [jax.ShapeDtypeStruct((tokens, QPG * DH), jnp.bfloat16)] * KVH
    kept = [(2 * DH, jnp.float32)]
    if offset == 0:
        wide = (QPG * DH, jnp.bfloat16)
        kept = [(2 * DH, jnp.bfloat16), wide, wide, wide] + kept
    return local_call(
        partial(backward_kernel, offset, planes, top_plane, first),
        shapes,
        5 * 2 * QPG * span * span * DH * 2,
        *kv,
        *q,
        *g,
        finals,
        *([] if first else [dq_old]),
        *passed,
        scratch=[pltpu.VMEM((span, width), kind) for width, kind in kept],
    )


def place_kernel(info, *refs):
    rank = info[1]
    sources, targets = refs[: 2 * KVH], refs[2 * KVH :]
    query_grad, key_grad, value_grad = targets
    for d in range(KVH):
        head = rank ^ d
        wide = pl.ds(pl.multiple_of(head * (QPG * DH), DH), QPG * DH)
        narrow = pl.ds(pl.multiple_of(head * DH, DH), DH)
        query_grad[:, wide] = sources[d][...]
        key_grad[:, narrow] = sources[KVH + d][:, :DH]
        value_grad[:, narrow] = sources[KVH + d][:, DH:]


def place_call(dq, dkv):
    tokens = dq[0].shape[0]
    shapes = [
        jax.ShapeDtypeStruct((tokens, KVH * QPG * DH), jnp.bfloat16),
        jax.ShapeDtypeStruct((tokens, KVH * DH), jnp.bfloat16),
        jax.ShapeDtypeStruct((tokens, KVH * DH), jnp.bfloat16),
    ]
    return local_call(place_kernel, shapes, 0, *dq, *dkv)


def per_device(queries, keys, values, out_grad):
    devices = lax.axis_size("seq")
    planes = devices // KVH
    tokens = queries.shape[0]
    device = lax.axis_index("seq")
    rank = device % KVH

    def swap(array, d):
        if d == 0:
            return array
        return lax.ppermute(array, "seq", [(i, i ^ d) for i in range(devices)])

    def columns(array, head, width):
        return lax.dynamic_slice_in_dim(array, head * width, width, axis=1)

    def after(array, *others):
        return lax.optimization_barrier((array,) + others)[0]

    kv_pieces = []
    for d in range(KVH):
        head = rank ^ d
        piece = jnp.concatenate([columns(keys, head, DH), columns(values, head, DH)], axis=1)
        kv_pieces.append(swap(piece, d))
    q_slices = [columns(queries, rank ^ d, QPG * DH) for d in range(KVH)]
    g_slices = [columns(out_grad, rank ^ d, QPG * DH) for d in range(KVH)]
    q = [swap(q_slices[d], d) for d in range(KVH)]
    g = [swap(g_slices[d], d) for d in range(KVH)]
    near = jnp.concatenate(kv_pieces[:2], axis=0)
    far = jnp.concatenate([after(kv_pieces[2], near, *q_slices), kv_pieces[3]], axis=0)
    chain = [(near, far)]
    for step in range(1, planes):
        pairs = [(i, i + KVH) for i in range((step - 1) * KVH, devices - KVH)]
        chain.append(tuple(lax.ppermute(half, "seq", pairs) for half in chain[-1]))
    state = []
    for offset in range(planes - 1):
        state = forward_call(offset, planes, chain[offset], q, g, state)
    finals, state = state[0], state[1:]
    arrived = []

    def gradients(top_plane, finals, passed):
        dq = None
        start = planes - 1 if top_plane else planes - 2
        for offset in reversed(range(start + 1)):
            kv = chain[offset]
            if top_plane and offset == 0:
                kv = (after(kv[0], *arrived[: planes - 2]), kv[1])
            if offset == planes - 2 and not top_plane:
                kv = (after(kv[0], *chain[-1]), kv[1])
            results = backward_call(
                offset,
                planes,
                top_plane,
                kv,
                q,
                g,
                finals,
                dq,
                passed if offset == 0 else [],
            )
            if offset == 0:
                return results
            senders = range(devices - KVH, devices) if top_plane else range(offset * KVH, devices - KVH)
            pairs = [(i, i - offset * KVH) for i in senders]
            arrived.append(lax.ppermute(results[0], "seq", pairs))
            dq = results[1]

    lower = gradients(False, finals, [])
    top_kv = (after(chain[-1][0], lower[1]), chain[-1][1])
    finals = forward_call(planes - 1, planes, top_kv, q, g, state)[0]
    results = gradients(True, finals, lower)
    total, dq = results[0], results[1:]
    for part in arrived:
        total = total + part.astype(jnp.float32)
    total = total.astype(jnp.bfloat16)
    dq = [dq[0], after(dq[1], arrived[planes - 2])] + list(dq[2:])
    dq_back = [swap(dq[d], d) for d in range(KVH)]
    dkv_back = [swap(total[d * tokens : (d + 1) * tokens], d) for d in range(KVH)]
    return tuple(place_call(dq_back, dkv_back))


def solution(mesh):
    spec = P(("groups", "seq"), None)
    return jax.shard_map(
        per_device,
        mesh=mesh,
        in_specs=(spec,) * 4,
        out_specs=(spec,) * 3,
        check_vma=False,
    )
```

```python
from functools import partial

import jax
import jax.numpy as jnp
from jax import lax
from jax.experimental import pallas as pl
from jax.experimental.pallas import tpu as pltpu
from jax.sharding import PartitionSpec as P

DH = 128
KVH = 4
QPG = 5
SCALING = DH ** (-0.5)
LOG2E = 1.4426950408889634
CONTRACT_LAST = (((1,), (1,)), ((), ()))
VMEM_BYTES = 28 * 1024 * 1024
EXTRA = 8


def token_places(rank, tokens, dim):
    shape = (tokens, 1) if dim == 0 else (1, tokens)
    own = lax.broadcasted_iota(jnp.int32, shape, dim)
    return jnp.concatenate([own + tokens * (rank ^ d) for d in range(KVH)], axis=dim)


def causal_mask(info, tokens):
    return token_places(info[1], tokens, 0) <= token_places(info[1], tokens, 1)


def stacked(refs, head):
    return jnp.concatenate([ref[:, head * DH : (head + 1) * DH] for ref in refs], axis=0)


def keys_values(refs):
    return (
        jnp.concatenate([ref[:, :DH] for ref in refs], axis=0),
        jnp.concatenate([ref[:, DH:] for ref in refs], axis=0),
    )


def scaled_scores(key_rows, query_rows):
    raw = lax.dot_general(key_rows, query_rows, CONTRACT_LAST, preferred_element_type=jnp.float32)
    return raw * (SCALING * LOG2E)


def forward_kernel(offset, planes, info, *refs):
    refs = list(refs)
    kv = [refs.pop(0) for _ in range(2)]
    q = [refs.pop(0) for _ in range(KVH)]
    top_plane = offset == planes - 1
    closes = offset >= planes - 2
    g = [refs.pop(0) for _ in range(KVH)] if closes else None
    if offset:
        old_stats, old_sums = refs.pop(0), refs.pop(0)
    finals = refs.pop(0) if closes else None
    stats, sums = refs
    tokens = q[0].shape[0]

    def update():
        key_rows, value_rows = keys_values(kv)
        span = key_rows.shape[0]
        left = jnp.concatenate([value_rows.T, jnp.ones((EXTRA, span), jnp.bfloat16)], axis=0)
        mask = None if offset else causal_mask(info, tokens)
        scores = []
        for h in range(QPG):
            raw = scaled_scores(key_rows, stacked(q, h))
            scores.append(raw if offset else jnp.where(mask, raw, -jnp.inf))
        tops = [jnp.max(raw, axis=0, keepdims=True) for raw in scores]
        for h in range(QPG):
            top = tops[h]
            if offset:
                old_top = old_stats[h, 0:1]
                top = jnp.maximum(old_top, top)
            weights = jnp.exp2(scores[h] - top).astype(jnp.bfloat16)
            added = jnp.dot(left, weights, preferred_element_type=jnp.float32)
            if offset:
                added = added + jnp.exp2(old_top - top) * old_sums[h]
            stats[h, 0:1] = top
            sums[h] = added

    def close():
        for h in range(QPG):
            grads = stacked(g, h).T.astype(jnp.float32)
            weighted = jnp.sum(sums[h, :DH] * grads, axis=0, keepdims=True)
            total = sums[h, DH : DH + 1]
            finals[h, 0:1] = stats[h, 0:1] + jnp.log2(total)
            finals[h, 1:2] = weighted / total

    if offset == 0:
        update()
    else:
        pl.when(info[0] >= offset)(update)
    if offset and not top_plane:

        @pl.when(info[0] < offset)
        def _():
            stats[...] = old_stats[...]
            sums[...] = old_sums[...]

    if closes:
        pl.when((info[0] == planes - 1) == top_plane)(close)


def backward_kernel(offset, planes, top_plane, first, info, *refs):
    refs = list(refs)
    plane = info[0]
    kv = [refs.pop(0) for _ in range(2)]
    q = [refs.pop(0) for _ in range(KVH)]
    g = [refs.pop(0) for _ in range(KVH)]
    finals = refs.pop(0)
    dq_old = None if first else refs.pop(0)
    own = offset == 0
    passed = [refs.pop(0) for _ in range(1 + KVH)] if own and top_plane else None
    dkv = refs.pop(0)
    gathered = None if own else refs.pop()
    ordered = refs[-5:] if own else None
    dq_refs = refs[:-5] if own else refs
    tokens = q[0].shape[0]

    def work():
        key_rows, value_rows = keys_values(kv)
        key_columns = key_rows.T
        for h in range(QPG):
            query_rows = stacked(q, h)
            grad_rows = stacked(g, h)
            probs = jnp.exp2(scaled_scores(key_rows, query_rows) - finals[h, 0:1])
            grad_probs = lax.dot_general(
                value_rows, grad_rows, CONTRACT_LAST, preferred_element_type=jnp.float32
            )
            grad_scores = (probs * (grad_probs - finals[h, 1:2]) * SCALING).astype(jnp.bfloat16)
            dk = jnp.dot(grad_scores, query_rows, preferred_element_type=jnp.float32)
            dv = jnp.dot(
                probs.astype(jnp.bfloat16), grad_rows, preferred_element_type=jnp.float32
            )
            if h == 0:
                gathered[:, :DH] = dk
                gathered[:, DH:] = dv
            else:
                gathered[:, :DH] += dk
                gathered[:, DH:] += dv
            dq = jnp.dot(key_columns, grad_scores, preferred_element_type=jnp.float32)
            if dq_old is not None:
                earlier = dq_old[h]
                if not top_plane:
                    earlier = jnp.where(plane > offset, earlier, 0.0)
                dq = dq + earlier
            dq_refs[0][h] = dq
        dkv[...] = gathered[...].astype(dkv.dtype)

    def own_work():
        rank = info[1]

        def place(j):
            return pl.ds(pl.multiple_of((j ^ rank) * tokens, tokens), tokens)

        def in_order(ref, h, row, rows):
            return jnp.concatenate(
                [ref[h, row : row + rows, place(j)] for j in range(KVH)], axis=1
            )

        kv_rows, q_rows, g_rows, dq_rows, dkv_rows = ordered
        for d in range(KVH):
            half = kv[d // 2]
            kv_rows[place(d), :] = half[d % 2 * tokens : (d % 2 + 1) * tokens, :]
            q_rows[place(d), :] = q[d][...]
            g_rows[place(d), :] = g[d][...]
        span = KVH * tokens
        half = span // 2
        masks = []
        for part in range(2):
            shape = (half * (part + 1), half)
            key_at = lax.broadcasted_iota(jnp.int32, shape, 0)
            masks.append(key_at <= lax.broadcasted_iota(jnp.int32, shape, 1) + part * half)
        key_columns = kv_rows[:, :DH].T
        for h in range(QPG):
            columns = slice(h * DH, (h + 1) * DH)
            log_total = in_order(finals, h, 0, 1)
            row_delta = in_order(finals, h, 1, 1)
            earlier = None
            if dq_old is not None:
                earlier = in_order(dq_old, h, 0, DH)
                if not top_plane:
                    earlier = jnp.where(plane > offset, earlier, 0.0)
            for part in range(2):
                reach = half * (part + 1)
                lanes = slice(part * half, (part + 1) * half)
                query_rows = q_rows[lanes, columns]
                grad_rows = g_rows[lanes, columns]
                scores = scaled_scores(kv_rows[:reach, :DH], query_rows)
                probs = jnp.exp2(scores - log_total[:, lanes])
                probs = jnp.where(masks[part], probs, 0.0)
                grad_probs = lax.dot_general(
                    kv_rows[:reach, DH:],
                    grad_rows,
                    CONTRACT_LAST,
                    preferred_element_type=jnp.float32,
                )
                grad_scores = (probs * (grad_probs - row_delta[:, lanes]) * SCALING).astype(
                    jnp.bfloat16
                )
                dk = jnp.dot(grad_scores, query_rows, preferred_element_type=jnp.float32)
                dv = jnp.dot(
                    probs.astype(jnp.bfloat16), grad_rows, preferred_element_type=jnp.float32
                )
                if h == 0 and part == 0:
                    dkv_rows[:reach, :DH] = dk
                    dkv_rows[:reach, DH:] = dv
                elif h == 0:
                    dkv_rows[:half, :DH] += dk[:half]
                    dkv_rows[:half, DH:] += dv[:half]
                    dkv_rows[half:, :DH] = dk[half:]
                    dkv_rows[half:, DH:] = dv[half:]
                else:
                    dkv_rows[:reach, :DH] += dk
                    dkv_rows[:reach, DH:] += dv
                dq = jnp.dot(
                    key_columns[:, :reach], grad_scores, preferred_element_type=jnp.float32
                )
                if earlier is not None:
                    dq = dq + earlier[:, lanes]
                dq_rows[lanes, columns] = dq.T.astype(jnp.bfloat16)
        for d in range(KVH):
            dq_refs[d][...] = dq_rows[place(d), :]
            dkv[d * tokens : (d + 1) * tokens, :] = dkv_rows[place(d), :]

    if own:
        work = own_work
    if top_plane:
        pl.when(plane == planes - 1)(work)
        if own:

            @pl.when(plane < planes - 1)
            def _():
                for source, target in zip(passed, [dkv] + dq_refs):
                    target[...] = source[...]
    else:
        pl.when((plane >= offset) & (plane < planes - 1))(work)


def local_call(kernel, shapes, flops, *operands, scratch=()):
    vmem = pl.BlockSpec(memory_space=pltpu.VMEM)

    def placed(*refs):
        device = lax.axis_index("seq")
        kernel((lax.div(device, KVH), lax.rem(device, KVH)), *refs)

    return pl.pallas_call(
        placed,
        in_specs=[vmem] * len(operands),
        out_specs=[vmem] * len(shapes),
        out_shape=shapes,
        scratch_shapes=scratch,
        compiler_params=pltpu.CompilerParams(vmem_limit_bytes=VMEM_BYTES),
        cost_estimate=pl.CostEstimate(flops=flops // 10, bytes_accessed=0, transcendentals=0),
    )(*operands)


def forward_call(offset, planes, kv, q, g, state):
    tokens = q[0].shape[0]
    span = KVH * tokens
    stats = jax.ShapeDtypeStruct((QPG, 8, span), jnp.float32)
    sums = jax.ShapeDtypeStruct((QPG, DH + EXTRA, span), jnp.float32)
    top_plane = offset == planes - 1
    closes = offset >= planes - 2
    shapes = [stats] * closes + [stats, sums] * (not top_plane)
    kept = [pltpu.VMEM(part.shape, part.dtype) for part in (stats, sums)] * top_plane
    return local_call(
        partial(forward_kernel, offset, planes),
        shapes,
        2 * 2 * QPG * span * span * DH * 2,
        *kv,
        *q,
        *(g if closes else []),
        *state,
        scratch=kept,
    )


def backward_call(offset, planes, top_plane, kv, q, g, finals, dq_old, passed):
    tokens = q[0].shape[0]
    span = KVH * tokens
    first = dq_old is None
    kind = jnp.bfloat16 if offset else jnp.float32
    shapes = [jax.ShapeDtypeStruct((span, 2 * DH), kind)]
    if offset:
        shapes += [jax.ShapeDtypeStruct((QPG, DH, span), jnp.float32)]
    else:
        shapes += [jax.ShapeDtypeStruct((tokens, QPG * DH), jnp.bfloat16)] * KVH
    kept = [(2 * DH, jnp.float32)]
    if offset == 0:
        wide = (QPG * DH, jnp.bfloat16)
        kept = [(2 * DH, jnp.bfloat16), wide, wide, wide] + kept
    return local_call(
        partial(backward_kernel, offset, planes, top_plane, first),
        shapes,
        5 * 2 * QPG * span * span * DH * 2,
        *kv,
        *q,
        *g,
        finals,
        *([] if first else [dq_old]),
        *passed,
        scratch=[pltpu.VMEM((span, width), kind) for width, kind in kept],
    )


def place_kernel(info, *refs):
    rank = info[1]
    sources, targets = refs[: 2 * KVH], refs[2 * KVH :]
    query_grad, key_grad, value_grad = targets
    for d in range(KVH):
        head = rank ^ d
        wide = pl.ds(pl.multiple_of(head * (QPG * DH), DH), QPG * DH)
        narrow = pl.ds(pl.multiple_of(head * DH, DH), DH)
        query_grad[:, wide] = sources[d][...]
        key_grad[:, narrow] = sources[KVH + d][:, :DH]
        value_grad[:, narrow] = sources[KVH + d][:, DH:]


def place_call(dq, dkv):
    tokens = dq[0].shape[0]
    shapes = [
        jax.ShapeDtypeStruct((tokens, KVH * QPG * DH), jnp.bfloat16),
        jax.ShapeDtypeStruct((tokens, KVH * DH), jnp.bfloat16),
        jax.ShapeDtypeStruct((tokens, KVH * DH), jnp.bfloat16),
    ]
    return local_call(place_kernel, shapes, 0, *dq, *dkv)


def per_device(queries, keys, values, out_grad):
    devices = lax.axis_size("seq")
    planes = devices // KVH
    tokens = queries.shape[0]
    device = lax.axis_index("seq")
    rank = device % KVH

    def swap(array, d):
        if d == 0:
            return array
        return lax.ppermute(array, "seq", [(i, i ^ d) for i in range(devices)])

    def columns(array, head, width):
        return lax.dynamic_slice_in_dim(array, head * width, width, axis=1)

    def after(array, *others):
        return lax.optimization_barrier((array,) + others)[0]

    kv_pieces = []
    for d in range(KVH):
        head = rank ^ d
        piece = jnp.concatenate([columns(keys, head, DH), columns(values, head, DH)], axis=1)
        kv_pieces.append(swap(piece, d))
    q_slices = [columns(queries, rank ^ d, QPG * DH) for d in range(KVH)]
    g_slices = [columns(out_grad, rank ^ d, QPG * DH) for d in range(KVH)]
    q = [swap(q_slices[d], d) for d in range(KVH)]
    g = [swap(g_slices[d], d) for d in range(KVH)]
    near = jnp.concatenate(kv_pieces[:2], axis=0)
    far = jnp.concatenate([after(kv_pieces[2], near, *q_slices), kv_pieces[3]], axis=0)
    chain = [(near, far)]
    for step in range(1, planes):
        pairs = [(i, i + KVH) for i in range((step - 1) * KVH, devices - KVH)]
        chain.append(tuple(lax.ppermute(half, "seq", pairs) for half in chain[-1]))
    state = []
    for offset in range(planes - 1):
        state = forward_call(offset, planes, chain[offset], q, g, state)
    finals, state = state[0], state[1:]
    arrived = []

    def gradients(top_plane, finals, passed):
        dq = None
        start = planes - 1 if top_plane else planes - 2
        for offset in reversed(range(start + 1)):
            kv = chain[offset]
            if top_plane and offset == 0:
                kv = (after(kv[0], arrived[0]), kv[1])
            if offset == planes - 2 and not top_plane:
                kv = (after(kv[0], *chain[-1]), kv[1])
            results = backward_call(
                offset,
                planes,
                top_plane,
                kv,
                q,
                g,
                finals,
                dq,
                passed if offset == 0 else [],
            )
            if offset == 0:
                return results
            senders = range(devices - KVH, devices) if top_plane else range(offset * KVH, devices - KVH)
            pairs = [(i, i - offset * KVH) for i in senders]
            arrived.append(lax.ppermute(results[0], "seq", pairs))
            dq = results[1]

    lower = gradients(False, finals, [])
    top_kv = (after(chain[-1][0], lower[1]), chain[-1][1])
    finals = forward_call(planes - 1, planes, top_kv, q, g, state)[0]
    results = gradients(True, finals, lower)
    total, dq = results[0], results[1:]
    for part in arrived:
        total = total + part.astype(jnp.float32)
    total = total.astype(jnp.bfloat16)
    dq = [dq[0], after(dq[1], *arrived[1 : planes - 1])] + list(dq[2:])
    dq_back = [swap(dq[d], d) for d in range(KVH)]
    dkv_back = [swap(total[d * tokens : (d + 1) * tokens], d) for d in range(KVH)]
    return tuple(place_call(dq_back, dkv_back))


def solution(mesh):
    spec = P(("groups", "seq"), None)
    return jax.shard_map(
        per_device,
        mesh=mesh,
        in_specs=(spec,) * 4,
        out_specs=(spec,) * 3,
        check_vma=False,
    )
```
